32 devices in a mesh: groups: 2 (over y), nodes: 16 (over z, x, core).
Axes of the slice: x: 2, y: 2, z: 4, core: 2. Of those that a mesh axis runs over, the one named last changes fastest.
Arguments:
- grid_latents: bfloat16 [32768, 1024], P(('groups', 'nodes')), parts along dimension 0, may hold values from -16 to 16
- mesh_latents: bfloat16 [8192, 1024], P(('groups', 'nodes')), parts along dimension 0, may hold values from -16 to 16
- neighbour_tiles: int32 [32, 6], P('nodes'), may hold values from 0 to 127, as said below
- neighbour_live: int32 [32, 6], P('nodes'), may hold values from 0 to 1, as said below
- w_query: bfloat16 [1024, 1024], replicated, may hold values from -0.1875 to 0.1875
- w_keyval: bfloat16 [1024, 2048], replicated, may hold values from -0.1875 to 0.1875
- w_out: bfloat16 [1024, 1024], replicated, may hold values from -0.375 to 0.375
Outputs:
- mesh_next: float32 [8192, 1024], P(('groups', 'nodes')), parts along dimension 0
The draws below stay inside these ranges and needn't reach their ends.
There are 2 independent parts, one for each index of `groups`. The reference program is written for one: setup_inputs(seed, part) draws one part's arguments, and reference() takes and returns one part's arrays. A program takes and returns all parts, laid end to end along the dimension named above; an argument that names none is the same for every part. Nothing has to cross between parts.
Inputs may be any that keep to these rules, and one draw needn't show every extreme that they name: `neighbour_tiles`: tile t lies on device t // 8 along nodes and mesh tile m on device m // 2; every listed tile lies on a device at most 2 indices away cyclically. The 6 entries of one mesh tile are distinct. Among the live entries of one device's mesh tiles at most 2 distinct tiles come from any one other device, and on every device some other device gives exactly 2. `neighbour_live`: each mesh tile has 2 to 6 live entries.
All inputs are finite; a program needn't handle non-finite values.
Results may differ from the reference program's by a relative error of at most 0.002.
The reference program's roundings to bfloat16 on the way count: a program that leaves them out, or rounds other values in their place, can miss the bound.
Values may be sent and summed in bfloat16 or wider, within the bound.
A program may use at most 128 MiB of HBM per device.

```python
import jax
import jax.numpy as jnp
from jax import lax

C = 1024
HEADS = 16
TILE = 128
NB = 6
REACH = 2
CAP = 2
GT_DEV = 8
MT_DEV = 2
GRID = 16384
MESH = 4096
N_NODES = 16


def neighbour_plan(key):
    base = jax.random.fold_in(key, 7)
    key_sets, key_order, key_count, key_rank = jax.random.split(base, 4)
    node_total = N_NODES
    offset_count = 2 * REACH
    candidates = GT_DEV + offset_count * CAP
    spread = jnp.arange(GT_DEV, dtype=jnp.int32)
    set_scores = jax.random.randint(key_sets, (node_total, offset_count, GT_DEV), 0, 1 << 20) * GT_DEV + spread
    picked = jnp.argsort(set_scores, axis=-1)[:, :, :CAP].astype(jnp.int32)
    offsets = jnp.concatenate([jnp.arange(-REACH, 0), jnp.arange(1, REACH + 1)]).astype(jnp.int32)
    devices = jnp.arange(node_total, dtype=jnp.int32)
    sources = (devices[:, None] + offsets[None, :] + node_total) % node_total
    remote = sources[:, :, None] * GT_DEV + picked
    owned = devices[:, None] * GT_DEV + spread[None, :]
    pooled = jnp.concatenate([owned, remote.reshape(node_total, offset_count * CAP)], axis=1)
    columns = jnp.arange(candidates, dtype=jnp.int32)
    order_scores = jax.random.randint(key_order, (node_total, MT_DEV, candidates), 0, 1 << 20) * candidates + columns
    forced_low = GT_DEV + devices % offset_count * CAP
    forced = (columns[None, :] >= forced_low[:, None]) & (columns[None, :] < forced_low[:, None] + CAP)
    first_tile = (jnp.arange(MT_DEV) == 0)[None, :, None]
    order_scores = jnp.where(forced[:, None, :] & first_tile, (columns - candidates)[None, None, :], order_scores)
    ordering = jnp.argsort(order_scores, axis=-1)[:, :, :NB]
    spread_pool = jnp.broadcast_to(pooled[:, None, :], (node_total, MT_DEV, candidates))
    tiles = jnp.take_along_axis(spread_pool, ordering, axis=-1)
    live_count = jax.random.randint(key_count, (node_total, MT_DEV), 2, NB + 1)
    live_count = jnp.where(jnp.arange(MT_DEV)[None, :] == 0, jnp.maximum(live_count, CAP), live_count)
    slot_ids = jnp.arange(NB, dtype=jnp.int32)
    rank_scores = jax.random.randint(key_rank, (node_total, MT_DEV, NB), 0, 1 << 20) * NB + slot_ids
    first_slots = first_tile & (slot_ids < CAP)[None, None, :]
    rank_scores = jnp.where(first_slots, (slot_ids - NB)[None, None, :], rank_scores)
    ranks = jnp.argsort(jnp.argsort(rank_scores, axis=-1), axis=-1)
    live = (ranks < live_count[:, :, None]).astype(jnp.int32)
    return (tiles.reshape(node_total * MT_DEV, NB).astype(jnp.int32), live.reshape(node_total * MT_DEV, NB))


def draw_neighbour_tiles(key, part):
    return neighbour_plan(key)[0]


def draw_neighbour_live(key, part):
    return neighbour_plan(key)[1]


def draw_grid_latents(key, part):
    key_values = jax.random.fold_in(jax.random.fold_in(key, 11), 0)
    values = jnp.clip(jax.random.normal(key_values, (GRID, C)), -6.0, 6.0)
    return values.astype(jnp.float32).astype(jnp.bfloat16)


def draw_mesh_latents(key, part):
    key_values = jax.random.fold_in(jax.random.fold_in(key, 13), 0)
    values = jnp.clip(2.0 * jax.random.normal(key_values, (MESH, C)), -12.0, 12.0)
    return values.astype(jnp.float32).astype(jnp.bfloat16)


def scatter_about(key, dims, scale, bound, held_as=jnp.bfloat16):
    return jnp.clip(scale * jax.random.normal(key, dims, jnp.float32), -bound, bound).astype(held_as)


def setup_inputs(seed: int = 0, part: int = 0) -> dict:
    streams_of = jax.random.split(jax.random.key(seed), 8)
    own_keys = jax.random.split(jax.random.fold_in(streams_of[7], part), 8)
    grid_latents = draw_grid_latents(jax.random.fold_in(jax.random.fold_in(streams_of[7], part), 71), part)
    mesh_latents = draw_mesh_latents(jax.random.fold_in(jax.random.fold_in(streams_of[7], part), 71), part)
    neighbour_tiles = draw_neighbour_tiles(jax.random.fold_in(streams_of[7], 71), part)
    neighbour_live = draw_neighbour_live(jax.random.fold_in(streams_of[7], 71), part)
    w_query = scatter_about(streams_of[4], (C, C), C ** -0.5, 0.1875)
    w_keyval = scatter_about(streams_of[5], (C, 2 * C), C ** -0.5, 0.1875)
    w_out = scatter_about(streams_of[6], (C, C), (C // 4) ** -0.5, 0.375)
    return {"grid_latents": grid_latents, "mesh_latents": mesh_latents, "neighbour_tiles": neighbour_tiles, "neighbour_live": neighbour_live, "w_query": w_query, "w_keyval": w_keyval, "w_out": w_out}


def attend_tile(query_tile, chosen, live_list):
    model_width = query_tile.shape[1]
    head_size = model_width // HEADS
    key_rows = NB * TILE
    key_part = chosen[:, :, :model_width].reshape(key_rows, HEADS, head_size).astype(jnp.float32)
    value_part = chosen[:, :, model_width:].reshape(key_rows, HEADS, head_size).astype(jnp.float32)
    query_heads = query_tile.reshape(TILE, HEADS, head_size).astype(jnp.float32)
    scores = jnp.einsum('qhd,khd->hqk', query_heads, value_part * 0.0 + key_part) * (head_size ** -0.5)
    key_live = jnp.repeat(live_list > 0, TILE)
    scores = jnp.where(key_live[None, None, :], scores, -1e30)
    row_top = jnp.max(scores, axis=-1, keepdims=True)
    raised = jnp.exp(scores - row_top)
    row_total = jnp.sum(raised, axis=-1, keepdims=True)
    weights = (raised / row_total).astype(jnp.bfloat16)
    mixture = jnp.einsum('hqk,khd->qhd', weights.astype(jnp.float32), value_part)
    return mixture.astype(jnp.bfloat16).reshape(TILE, model_width)


def reference(grid_latents, mesh_latents, neighbour_tiles, neighbour_live, w_query, w_keyval, w_out):
    model_width = w_query.shape[0]
    grid_blocks = grid_latents.reshape(N_NODES, GT_DEV * TILE, model_width)

    def project_block(block):
        return jnp.dot(block, w_keyval, preferred_element_type=jnp.float32).astype(jnp.bfloat16)

    keyval = lax.map(project_block, grid_blocks).reshape(-1, TILE, 2 * model_width)
    queries = jnp.dot(mesh_latents, w_query, preferred_element_type=jnp.float32).astype(jnp.bfloat16)
    queries = queries.reshape(-1, TILE, model_width)

    def one_tile(inputs):
        query_tile, tile_list, live_list = inputs
        chosen = jnp.take(keyval, tile_list.astype(jnp.int32), axis=0)
        return attend_tile(query_tile, chosen, live_list)

    attended = lax.map(one_tile, (queries, neighbour_tiles, neighbour_live))
    attended = attended.reshape(-1, model_width)
    return mesh_latents.astype(jnp.float32) + jnp.dot(attended, w_out, preferred_element_type=jnp.float32)
```

```python
import functools

import jax
import jax.numpy as jnp
from jax import lax
from jax.experimental import pallas as pl
from jax.experimental.pallas import tpu as pltpu
from jax.sharding import PartitionSpec as P

HEADS = 16
TILE = 128
REACH = 2
CAP = 2
GROUP = 4
VMEM_LIMIT = 56 * 1024 * 1024


def plan_requests(tiles, live, own_tiles, offsets, position, node_count):
    owner = tiles // own_tiles
    local = tiles % own_tiles
    away = (owner - position + node_count + REACH) % node_count - REACH
    ids = jnp.arange(own_tiles, dtype=jnp.int32)
    slot_ids = jnp.arange(CAP, dtype=jnp.int32)
    requests = []
    table = jnp.where(away == 0, local, 0)
    for number, offset in enumerate(offsets):
        wanted = (live > 0) & (away == offset)
        needed = jnp.any(wanted[:, :, None] & (local[:, :, None] == ids), axis=(0, 1))
        before = jnp.sum(
            jnp.where(needed[None, :] & (ids[None, :] < ids[:, None]), 1, 0), axis=1
        )
        chosen = needed[None, :] & (before[None, :] == slot_ids[:, None])
        requests.append(jnp.sum(jnp.where(chosen, ids[None, :], 0), axis=1))
        place = jnp.sum(jnp.where(needed & (ids < local[:, :, None]), 1, 0), axis=2)
        table = jnp.where(wanted, own_tiles + number * CAP + place, table)
    return requests, table


def pick_kernel(request_ref, grid_ref, *refs):
    outs, sems = refs[:-1], refs[-1]
    copies = []
    for number, out in enumerate(outs):
        for slot in range(CAP):
            tile = request_ref[number * CAP + slot]
            copies.append(
                pltpu.make_async_copy(
                    grid_ref.at[tile], out.at[slot], sems.at[number * CAP + slot]
                )
            )
    for copy in copies:
        copy.start()
    for copy in copies:
        copy.wait()


def pick(requested, grid):
    count = requested.shape[0] // CAP
    return pl.pallas_call(
        pick_kernel,
        out_shape=[jax.ShapeDtypeStruct((CAP,) + grid.shape[1:], grid.dtype)] * count,
        in_specs=[
            pl.BlockSpec(memory_space=pltpu.SMEM),
            pl.BlockSpec(memory_space=pl.ANY),
        ],
        out_specs=[pl.BlockSpec(memory_space=pl.ANY)] * count,
        scratch_shapes=[pltpu.SemaphoreType.DMA((count * CAP,))],
        name="pick",
    )(requested, grid)


def encode_kernel(
    count, table_ref, live_ref, own_ref, w_keyval_ref, query_ref, w_out_ref, mesh_ref, *refs
):
    received = refs[:count]
    out_ref, keyval, attended, own_sem = refs[count:]
    own_tiles = own_ref.shape[0]
    tile_rows = keyval.shape[1]
    width = query_ref.shape[1]
    head_size = width // HEADS
    span = GROUP * head_size
    slots = table_ref.shape[1]
    mesh_tiles = table_ref.shape[0]

    own_copy = pltpu.make_async_copy(own_ref, keyval.at[0:own_tiles], own_sem)
    own_copy.start()
    for number, tiles in enumerate(received):
        rows = tiles[...].reshape(CAP * tile_rows, width)
        for part in range(0, 2 * width, 512):
            columns = slice(part, part + 512)
            done = jnp.dot(rows, w_keyval_ref[:, columns], preferred_element_type=jnp.float32)
            first = own_tiles + number * CAP
            keyval[first : first + CAP, :, columns] = done.astype(keyval.dtype).reshape(
                CAP, tile_rows, 512
            )
    own_copy.wait()

    lane_head = lax.broadcasted_iota(jnp.int32, (1, span), 1) // head_size
    key_slot = lax.broadcasted_iota(jnp.int32, (1, slots * tile_rows), 1) // tile_rows
    for tile in range(mesh_tiles):
        rows = slice(tile * tile_rows, (tile + 1) * tile_rows)
        bias = jnp.zeros((1, slots * tile_rows), jnp.float32)
        for slot in range(slots):
            off = jnp.where(live_ref[tile, slot] > 0, 0.0, -1e30)
            bias = jnp.where(key_slot == slot, off, bias)
        index = [table_ref[tile, slot] for slot in range(slots)]
        for group in range(HEADS // GROUP):
            columns = slice(group * span, (group + 1) * span)
            behind = slice(width + group * span, width + (group + 1) * span)
            query = query_ref[rows, columns]
            stacked = jnp.concatenate(
                [jnp.where(lane_head == h, query, jnp.zeros_like(query)) for h in range(GROUP)],
                axis=0,
            )
            keys = jnp.concatenate([keyval[i, :, columns] for i in index], axis=0)
            values = jnp.concatenate([keyval[i, :, behind] for i in index], axis=0)
            scores = lax.dot_general(
                stacked, keys, (((1,), (1,)), ((), ())), preferred_element_type=jnp.float32
            )
            scores = scores + bias
            raised = jnp.exp(scores - jnp.max(scores, axis=-1, keepdims=True))
            share = 1.0 / jnp.sum(raised, axis=-1, keepdims=True)
            weights = (raised * share).astype(jnp.bfloat16)
            mixed = jnp.dot(weights, values, preferred_element_type=jnp.float32)
            total = jnp.zeros((tile_rows, span), jnp.float32)
            for h in range(GROUP):
                total = jnp.where(
                    lane_head == h, mixed[h * tile_rows : (h + 1) * tile_rows], total
                )
            attended[rows, columns] = total.astype(jnp.bfloat16)
    for part in range(0, width, 512):
        columns = slice(part, part + 512)
        out_ref[:, columns] = mesh_ref[:, columns].astype(jnp.float32) + jnp.dot(
            attended[...], w_out_ref[:, columns], preferred_element_type=jnp.float32
        )


def encode(table, live, own, w_keyval, query, w_out, mesh_latents, received):
    count = len(received)
    own_tiles, tile_rows, wide = own.shape
    vmem = pl.BlockSpec(memory_space=pltpu.VMEM)
    smem = pl.BlockSpec(memory_space=pltpu.SMEM)
    return pl.pallas_call(
        functools.partial(encode_kernel, count),
        out_shape=jax.ShapeDtypeStruct(mesh_latents.shape, jnp.float32),
        in_specs=[smem, smem, pl.BlockSpec(memory_space=pl.ANY)] + [vmem] * (4 + count),
        out_specs=vmem,
        scratch_shapes=[
            pltpu.VMEM((own_tiles + count * CAP, tile_rows, wide), jnp.bfloat16),
            pltpu.VMEM(mesh_latents.shape, jnp.bfloat16),
            pltpu.SemaphoreType.DMA,
        ],
        compiler_params=pltpu.CompilerParams(vmem_limit_bytes=VMEM_LIMIT),
        name="encode",
    )(table, live, own, w_keyval, query, w_out, mesh_latents, *received)


def per_device(
    grid_latents, mesh_latents, neighbour_tiles, neighbour_live, w_query, w_keyval, w_out
):
    width = w_query.shape[0]
    own_tiles = grid_latents.shape[0] // TILE
    node_count = lax.axis_size("nodes")
    position = lax.axis_index("nodes")
    offsets = [o for o in range(-REACH, REACH + 1) if o != 0]

    def route(shift):
        return [(i, (i + shift) % node_count) for i in range(node_count)]

    requests, table = plan_requests(
        neighbour_tiles, neighbour_live, own_tiles, offsets, position, node_count
    )
    asked = [lax.ppermute(r, "nodes", route(o)) for r, o in zip(requests, offsets)]
    picked = pick(jnp.concatenate(asked), grid_latents.reshape(own_tiles, TILE, width))
    received = [lax.ppermute(p, "nodes", route(-o)) for p, o in zip(picked, offsets)]
    own = jnp.dot(grid_latents, w_keyval, preferred_element_type=jnp.float32)
    own = own.astype(jnp.bfloat16).reshape(own_tiles, TILE, 2 * width)
    scale = (width // HEADS) ** -0.5
    query = jnp.dot(mesh_latents, w_query, preferred_element_type=jnp.float32) * scale
    query = query.astype(jnp.bfloat16)
    return encode(
        table, neighbour_live, own, w_keyval, query, w_out, mesh_latents, received
    )


def solution(mesh):
    return jax.shard_map(
        per_device,
        mesh=mesh,
        in_specs=(
            P(("groups", "nodes"), None),
            P(("groups", "nodes"), None),
            P("nodes", None),
            P("nodes", None),
            P(),
            P(),
            P(),
        ),
        out_specs=P(("groups", "nodes"), None),
        check_vma=False,
    )
```

```python
import functools

import jax
import jax.numpy as jnp
from jax import lax
from jax.experimental import pallas as pl
from jax.experimental.pallas import tpu as pltpu
from jax.sharding import PartitionSpec as P

HEADS = 16
TILE = 128
REACH = 2
CAP = 2
GROUP = 4
VMEM_LIMIT = 56 * 1024 * 1024


def plan_requests(tiles, live, own_tiles, offsets, position, node_count):
    owner = tiles // own_tiles
    local = tiles % own_tiles
    away = (owner - position + node_count + REACH) % node_count - REACH
    ids = jnp.arange(own_tiles, dtype=jnp.int32)
    slot_ids = jnp.arange(CAP, dtype=jnp.int32)
    requests = []
    table = jnp.where(away == 0, local, 0)
    for number, offset in enumerate(offsets):
        wanted = (live > 0) & (away == offset)
        needed = jnp.any(wanted[:, :, None] & (local[:, :, None] == ids), axis=(0, 1))
        before = jnp.sum(
            jnp.where(needed[None, :] & (ids[None, :] < ids[:, None]), 1, 0), axis=1
        )
        chosen = needed[None, :] & (before[None, :] == slot_ids[:, None])
        requests.append(jnp.sum(jnp.where(chosen, ids[None, :], 0), axis=1))
        place = jnp.sum(jnp.where(needed & (ids < local[:, :, None]), 1, 0), axis=2)
        table = jnp.where(wanted, own_tiles + number * CAP + place, table)
    return requests, table


def pick_kernel(request_ref, grid_ref, *refs):
    outs, sems = refs[:-1], refs[-1]
    copies = []
    for number, out in enumerate(outs):
        for slot in range(CAP):
            tile = request_ref[number * CAP + slot]
            copies.append(
                pltpu.make_async_copy(
                    grid_ref.at[tile], out.at[slot], sems.at[number * CAP + slot]
                )
            )
    for copy in copies:
        copy.start()
    for copy in copies:
        copy.wait()


def pick(requested, grid):
    count = requested.shape[0] // CAP
    return pl.pallas_call(
        pick_kernel,
        out_shape=[jax.ShapeDtypeStruct((CAP,) + grid.shape[1:], grid.dtype)] * count,
        in_specs=[
            pl.BlockSpec(memory_space=pltpu.SMEM),
            pl.BlockSpec(memory_space=pl.ANY),
        ],
        out_specs=[pl.BlockSpec(memory_space=pltpu.VMEM)] * count,
        scratch_shapes=[pltpu.SemaphoreType.DMA((count * CAP,))],
        name="pick",
    )(requested, grid)


def encode_kernel(
    count, table_ref, live_ref, own_ref, w_keyval_ref, query_ref, w_out_ref, mesh_ref, *refs
):
    received = refs[:count]
    out_ref, keyval, attended, own_sem = refs[count:]
    own_tiles = own_ref.shape[0]
    tile_rows = keyval.shape[1]
    width = query_ref.shape[1]
    head_size = width // HEADS
    span = GROUP * head_size
    slots = table_ref.shape[1]
    mesh_tiles = table_ref.shape[0]

    own_copy = pltpu.make_async_copy(own_ref, keyval.at[0:own_tiles], own_sem)
    own_copy.start()
    for number, tiles in enumerate(received):
        rows = tiles[...].reshape(CAP * tile_rows, width)
        for part in range(0, 2 * width, 512):
            columns = slice(part, part + 512)
            done = jnp.dot(rows, w_keyval_ref[:, columns], preferred_element_type=jnp.float32)
            first = own_tiles + number * CAP
            keyval[first : first + CAP, :, columns] = done.astype(keyval.dtype).reshape(
                CAP, tile_rows, 512
            )
    own_copy.wait()

    lane_head = lax.broadcasted_iota(jnp.int32, (1, span), 1) // head_size
    key_slot = lax.broadcasted_iota(jnp.int32, (1, slots * tile_rows), 1) // tile_rows
    for tile in range(mesh_tiles):
        rows = slice(tile * tile_rows, (tile + 1) * tile_rows)
        bias = jnp.zeros((1, slots * tile_rows), jnp.float32)
        for slot in range(slots):
            off = jnp.where(live_ref[tile, slot] > 0, 0.0, -1e30)
            bias = jnp.where(key_slot == slot, off, bias)
        index = [table_ref[tile, slot] for slot in range(slots)]
        for group in range(HEADS // GROUP):
            columns = slice(group * span, (group + 1) * span)
            behind = slice(width + group * span, width + (group + 1) * span)
            query = query_ref[rows, columns]
            stacked = jnp.concatenate(
                [jnp.where(lane_head == h, query, jnp.zeros_like(query)) for h in range(GROUP)],
                axis=0,
            )
            keys = jnp.concatenate([keyval[i, :, columns] for i in index], axis=0)
            values = jnp.concatenate([keyval[i, :, behind] for i in index], axis=0)
            scores = lax.dot_general(
                stacked, keys, (((1,), (1,)), ((), ())), preferred_element_type=jnp.float32
            )
            scores = scores + bias
            raised = jnp.exp(scores - jnp.max(scores, axis=-1, keepdims=True))
            share = 1.0 / jnp.sum(raised, axis=-1, keepdims=True)
            weights = (raised * share).astype(jnp.bfloat16)
            mixed = jnp.dot(weights, values, preferred_element_type=jnp.float32)
            total = jnp.zeros((tile_rows, span), jnp.float32)
            for h in range(GROUP):
                total = jnp.where(
                    lane_head == h, mixed[h * tile_rows : (h + 1) * tile_rows], total
                )
            attended[rows, columns] = total.astype(jnp.bfloat16)
    for part in range(0, width, 512):
        columns = slice(part, part + 512)
        out_ref[:, columns] = mesh_ref[:, columns].astype(jnp.float32) + jnp.dot(
            attended[...], w_out_ref[:, columns], preferred_element_type=jnp.float32
        )


def encode(table, live, own, w_keyval, query, w_out, mesh_latents, received):
    count = len(received)
    own_tiles, tile_rows, wide = own.shape
    vmem = pl.BlockSpec(memory_space=pltpu.VMEM)
    smem = pl.BlockSpec(memory_space=pltpu.SMEM)
    return pl.pallas_call(
        functools.partial(encode_kernel, count),
        out_shape=jax.ShapeDtypeStruct(mesh_latents.shape, jnp.float32),
        in_specs=[smem, smem, pl.BlockSpec(memory_space=pl.ANY)] + [vmem] * (4 + count),
        out_specs=vmem,
        scratch_shapes=[
            pltpu.VMEM((own_tiles + count * CAP, tile_rows, wide), jnp.bfloat16),
            pltpu.VMEM(mesh_latents.shape, jnp.bfloat16),
            pltpu.SemaphoreType.DMA,
        ],
        compiler_params=pltpu.CompilerParams(vmem_limit_bytes=VMEM_LIMIT),
        name="encode",
    )(table, live, own, w_keyval, query, w_out, mesh_latents, *received)


def per_device(
    grid_latents, mesh_latents, neighbour_tiles, neighbour_live, w_query, w_keyval, w_out
):
    width = w_query.shape[0]
    own_tiles = grid_latents.shape[0] // TILE
    node_count = lax.axis_size("nodes")
    position = lax.axis_index("nodes")
    offsets = [o for o in range(-REACH, REACH + 1) if o != 0]

    def route(shift):
        return [(i, (i + shift) % node_count) for i in range(node_count)]

    requests, table = plan_requests(
        neighbour_tiles, neighbour_live, own_tiles, offsets, position, node_count
    )
    asked = [lax.ppermute(r, "nodes", route(o)) for r, o in zip(requests, offsets)]
    picked = pick(jnp.concatenate(asked), grid_latents.reshape(own_tiles, TILE, width))
    received = [lax.ppermute(p, "nodes", route(-o)) for p, o in zip(picked, offsets)]
    grid_latents, mesh_latents, _ = lax.optimization_barrier(
        (grid_latents, mesh_latents, picked)
    )
    own = jnp.dot(grid_latents, w_keyval, preferred_element_type=jnp.float32)
    own = own.astype(jnp.bfloat16).reshape(own_tiles, TILE, 2 * width)
    scale = (width // HEADS) ** -0.5
    query = jnp.dot(mesh_latents, w_query, preferred_element_type=jnp.float32) * scale
    query = query.astype(jnp.bfloat16)
    return encode(
        table, neighbour_live, own, w_keyval, query, w_out, mesh_latents, received
    )


def solution(mesh):
    return jax.shard_map(
        per_device,
        mesh=mesh,
        in_specs=(
            P(("groups", "nodes"), None),
            P(("groups", "nodes"), None),
            P("nodes", None),
            P("nodes", None),
            P(),
            P(),
            P(),
        ),
        out_specs=P(("groups", "nodes"), None),
        check_vma=False,
    )
```

```python
import functools

import jax
import jax.numpy as jnp
from jax import lax
from jax.experimental import pallas as pl
from jax.experimental.pallas import tpu as pltpu
from jax.sharding import PartitionSpec as P

HEADS = 16
TILE = 128
REACH = 2
CAP = 2
GROUP = 4
CHUNK = 256
VMEM_LIMIT = 44 * 1024 * 1024


def plan_requests(tiles, live, own_tiles, offsets, position, node_count):
    owner = tiles // own_tiles
    local = tiles % own_tiles
    away = (owner - position + node_count + REACH) % node_count - REACH
    ids = jnp.arange(own_tiles, dtype=jnp.int32)
    slot_ids = jnp.arange(CAP, dtype=jnp.int32)
    requests = []
    table = jnp.where(away == 0, local, 0)
    for number, offset in enumerate(offsets):
        wanted = (live > 0) & (away == offset)
        needed = jnp.any(wanted[:, :, None] & (local[:, :, None] == ids), axis=(0, 1))
        before = jnp.sum(
            jnp.where(needed[None, :] & (ids[None, :] < ids[:, None]), 1, 0), axis=1
        )
        chosen = needed[None, :] & (before[None, :] == slot_ids[:, None])
        requests.append(jnp.sum(jnp.where(chosen, ids[None, :], 0), axis=1))
        place = jnp.sum(jnp.where(needed & (ids < local[:, :, None]), 1, 0), axis=2)
        table = jnp.where(wanted, own_tiles + number * CAP + place, table)
    return requests, table


def shifted(offset):
    count = lax.axis_size("nodes")
    return lax.rem(lax.axis_index("nodes") + (offset + count), count)


def project(rows, weight_ref, store):
    @pl.loop(0, weight_ref.shape[1] // CHUNK)
    def _(step):
        columns = pl.ds(pl.multiple_of(step * CHUNK, CHUNK), CHUNK)
        store(
            columns,
            jnp.dot(rows(), weight_ref[:, columns], preferred_element_type=jnp.float32),
        )


def encode_kernel(
    offsets,
    request_ref,
    table_ref,
    live_ref,
    grid_ref,
    mesh_ref,
    w_query_hbm,
    w_keyval_hbm,
    w_out_hbm,
    out_ref,
    keyval,
    query_ref,
    attended,
    sending,
    received,
    w_query_ref,
    w_keyval_ref,
    w_out_ref,
    weight_sems,
    send_sems,
    recv_sems,
):
    own_tiles, tile_rows, width = grid_ref.shape
    head_size = width // HEADS
    span = GROUP * head_size
    mesh_tiles, slots = table_ref.shape

    loads = [
        pltpu.make_async_copy(source, target, weight_sems.at[number])
        for number, (source, target) in enumerate(
            (
                (w_keyval_hbm, w_keyval_ref),
                (w_query_hbm, w_query_ref),
                (w_out_hbm, w_out_ref),
            )
        )
    ]
    for load in loads:
        load.start()

    barrier = pltpu.get_barrier_semaphore()
    for offset in offsets:
        pl.semaphore_signal(
            barrier,
            inc=1,
            device_id={"nodes": shifted(offset)},
            device_id_type=pl.DeviceIdType.MESH,
        )
    pl.semaphore_wait(barrier, len(offsets))

    copies = []
    for number, offset in enumerate(offsets):
        for slot in range(CAP):
            sending[number, slot] = grid_ref[request_ref[number * CAP + slot]]
        copy = pltpu.make_async_remote_copy(
            src_ref=sending.at[number],
            dst_ref=received.at[number],
            send_sem=send_sems.at[number],
            recv_sem=recv_sems.at[number],
            device_id={"nodes": shifted(-offset)},
            device_id_type=pl.DeviceIdType.MESH,
        )
        copy.start()
        copies.append(copy)

    def keep(first, count):
        def store(columns, done):
            keyval[first : first + count, :, columns] = done.astype(keyval.dtype).reshape(
                count, tile_rows, CHUNK
            )

        return store

    loads[0].wait()
    project(
        lambda: grid_ref[...].reshape(own_tiles * tile_rows, width),
        w_keyval_ref,
        keep(0, own_tiles),
    )
    loads[1].wait()

    def store_query(columns, done):
        query_ref[:, columns] = (done * head_size ** (-0.5)).astype(query_ref.dtype)

    project(lambda: mesh_ref[...], w_query_ref, store_query)
    loads[2].wait()

    pair = 2
    for first in range(0, len(offsets), pair):
        for copy in copies[first : first + pair]:
            copy.wait()
        project(
            lambda: received[first : first + pair].reshape(pair * CAP * tile_rows, width),
            w_keyval_ref,
            keep(own_tiles + first * CAP, pair * CAP),
        )

    lane_head = lax.broadcasted_iota(jnp.int32, (1, span), 1) // head_size
    key_slot = lax.broadcasted_iota(jnp.int32, (1, slots * tile_rows), 1) // tile_rows
    for tile in range(mesh_tiles):
        rows = slice(tile * tile_rows, (tile + 1) * tile_rows)
        bias = jnp.zeros((1, slots * tile_rows), jnp.float32)
        for slot in range(slots):
            off = jnp.where(live_ref[tile, slot] > 0, 0.0, -1e30)
            bias = jnp.where(key_slot == slot, off, bias)
        index = [table_ref[tile, slot] for slot in range(slots)]
        for group in range(HEADS // GROUP):
            columns = slice(group * span, (group + 1) * span)
            behind = slice(width + group * span, width + (group + 1) * span)
            query = query_ref[rows, columns]
            stacked = jnp.concatenate(
                [jnp.where(lane_head == h, query, jnp.zeros_like(query)) for h in range(GROUP)],
                axis=0,
            )
            keys = jnp.concatenate([keyval[i, :, columns] for i in index], axis=0)
            values = jnp.concatenate([keyval[i, :, behind] for i in index], axis=0)
            scores = lax.dot_general(
                stacked, keys, (((1,), (1,)), ((), ())), preferred_element_type=jnp.float32
            )
            scores = scores + bias
            raised = jnp.exp(scores - jnp.max(scores, axis=-1, keepdims=True))
            share = 1.0 / jnp.sum(raised, axis=-1, keepdims=True)
            weights = (raised * share).astype(jnp.bfloat16)
            mixed = jnp.dot(weights, values, preferred_element_type=jnp.float32)
            total = jnp.zeros((tile_rows, span), jnp.float32)
            for h in range(GROUP):
                total = jnp.where(
                    lane_head == h, mixed[h * tile_rows : (h + 1) * tile_rows], total
                )
            attended[rows, columns] = total.astype(jnp.bfloat16)
    for part in range(0, width, 512):
        columns = slice(part, part + 512)
        out_ref[:, columns] = mesh_ref[:, columns].astype(jnp.float32) + jnp.dot(
            attended[...], w_out_ref[:, columns], preferred_element_type=jnp.float32
        )


def encode(offsets, request, table, live, grid, mesh_latents, w_query, w_keyval, w_out):
    own_tiles, tile_rows, width = grid.shape
    count = len(offsets)
    vmem = pl.BlockSpec(memory_space=pltpu.VMEM)
    smem = pl.BlockSpec(memory_space=pltpu.SMEM)
    hbm = pl.BlockSpec(memory_space=pl.ANY)
    bf16 = jnp.bfloat16
    return pl.pallas_call(
        functools.partial(encode_kernel, offsets),
        out_shape=jax.ShapeDtypeStruct(mesh_latents.shape, jnp.float32),
        in_specs=[smem, smem, smem, vmem, vmem, hbm, hbm, hbm],
        out_specs=vmem,
        scratch_shapes=[
            pltpu.VMEM((own_tiles + count * CAP, tile_rows, 2 * width), bf16),
            pltpu.VMEM(mesh_latents.shape, bf16),
            pltpu.VMEM(mesh_latents.shape, bf16),
            pltpu.VMEM((count, CAP, tile_rows, width), bf16),
            pltpu.VMEM((count, CAP, tile_rows, width), bf16),
            pltpu.VMEM(w_query.shape, bf16),
            pltpu.VMEM(w_keyval.shape, bf16),
            pltpu.VMEM(w_out.shape, bf16),
            pltpu.SemaphoreType.DMA((3,)),
            pltpu.SemaphoreType.DMA((count,)),
            pltpu.SemaphoreType.DMA((count,)),
        ],
        compiler_params=pltpu.CompilerParams(
            vmem_limit_bytes=VMEM_LIMIT, collective_id=0, has_side_effects=True
        ),
        name="encode",
    )(request, table, live, grid, mesh_latents, w_query, w_keyval, w_out)


def per_device(
    grid_latents, mesh_latents, neighbour_tiles, neighbour_live, w_query, w_keyval, w_out
):
    width = w_query.shape[0]
    own_tiles = grid_latents.shape[0] // TILE
    node_count = lax.axis_size("nodes")
    position = lax.axis_index("nodes")
    offsets = [sign * o for o in range(1, REACH + 1) for sign in (-1, 1)]

    def route(shift):
        return [(i, (i + shift) % node_count) for i in range(node_count)]

    requests, table = plan_requests(
        neighbour_tiles, neighbour_live, own_tiles, offsets, position, node_count
    )
    asked = [lax.ppermute(r, "nodes", route(o)) for r, o in zip(requests, offsets)]
    return encode(
        offsets,
        jnp.concatenate(asked),
        table,
        neighbour_live,
        grid_latents.reshape(own_tiles, TILE, width),
        mesh_latents,
        w_query,
        w_keyval,
        w_out,
    )


def solution(mesh):
    return jax.shard_map(
        per_device,
        mesh=mesh,
        in_specs=(
            P(("groups", "nodes"), None),
            P(("groups", "nodes"), None),
            P("nodes", None),
            P("nodes", None),
            P(),
            P(),
            P(),
        ),
        out_specs=P(("groups", "nodes"), None),
        check_vma=False,
    )
```

```python
import functools

import jax
import jax.numpy as jnp
from jax import lax
from jax.experimental import pallas as pl
from jax.experimental.pallas import tpu as pltpu
from jax.sharding import PartitionSpec as P

HEADS = 16
TILE = 128
REACH = 2
CAP = 2
GROUP = 4
CHUNK = 256
VMEM_LIMIT = 60 * 1024 * 1024


def plan_requests(tiles, live, own_tiles, offsets, position, node_count):
    owner = tiles // own_tiles
    local = tiles % own_tiles
    away = (owner - position + node_count + REACH) % node_count - REACH
    ids = jnp.arange(own_tiles, dtype=jnp.int32)
    slot_ids = jnp.arange(CAP, dtype=jnp.int32)
    requests = []
    table = jnp.where(away == 0, local, 0)
    for number, offset in enumerate(offsets):
        wanted = (live > 0) & (away == offset)
        needed = jnp.any(wanted[:, :, None] & (local[:, :, None] == ids), axis=(0, 1))
        before = jnp.sum(
            jnp.where(needed[None, :] & (ids[None, :] < ids[:, None]), 1, 0), axis=1
        )
        chosen = needed[None, :] & (before[None, :] == slot_ids[:, None])
        requests.append(jnp.sum(jnp.where(chosen, ids[None, :], 0), axis=1))
        place = jnp.sum(jnp.where(needed & (ids < local[:, :, None]), 1, 0), axis=2)
        table = jnp.where(wanted, own_tiles + number * CAP + place, table)
    return requests, table


def shifted(offset):
    count = lax.axis_size("nodes")
    return lax.rem(lax.axis_index("nodes") + (offset + count), count)


def project(rows, weight_ref, store):
    @pl.loop(0, weight_ref.shape[1] // CHUNK)
    def _(step):
        columns = pl.ds(pl.multiple_of(step * CHUNK, CHUNK), CHUNK)
        store(
            columns,
            jnp.dot(rows(), weight_ref[:, columns], preferred_element_type=jnp.float32),
        )


def encode_kernel(
    offsets,
    request_ref,
    table_ref,
    live_ref,
    grid_ref,
    mesh_ref,
    w_query_hbm,
    w_keyval_hbm,
    w_out_hbm,
    out_ref,
    keyval,
    query_ref,
    attended,
    sending,
    received,
    w_query_ref,
    w_keyval_ref,
    w_out_ref,
    asked_ref,
    asked_smem,
    weight_sems,
    send_sems,
    recv_sems,
    ask_send_sems,
    ask_recv_sems,
    ask_sems,
):
    own_tiles, tile_rows, width = grid_ref.shape
    head_size = width // HEADS
    span = GROUP * head_size
    mesh_tiles, slots = table_ref.shape

    loads = [
        pltpu.make_async_copy(source, target, weight_sems.at[number])
        for number, (source, target) in enumerate(
            (
                (w_query_hbm, w_query_ref),
                (w_keyval_hbm, w_keyval_ref),
                (w_out_hbm, w_out_ref),
            )
        )
    ]
    for load in loads:
        load.start()

    barrier = pltpu.get_barrier_semaphore()
    for offset in offsets:
        pl.semaphore_signal(
            barrier,
            inc=1,
            device_id={"nodes": shifted(offset)},
            device_id_type=pl.DeviceIdType.MESH,
        )
    pl.semaphore_wait(barrier, len(offsets))

    asks = []
    for number, offset in enumerate(offsets):
        ask = pltpu.make_async_remote_copy(
            src_ref=request_ref.at[number],
            dst_ref=asked_ref.at[number],
            send_sem=ask_send_sems.at[number],
            recv_sem=ask_recv_sems.at[number],
            device_id={"nodes": shifted(offset)},
            device_id_type=pl.DeviceIdType.MESH,
        )
        ask.start()
        asks.append(ask)

    loads[0].wait()

    def store_query(columns, done):
        query_ref[:, columns] = (done * head_size ** (-0.5)).astype(query_ref.dtype)

    project(lambda: mesh_ref[...], w_query_ref, store_query)

    copies = []
    for number, offset in enumerate(offsets):
        asks[number].wait()
        fetch = pltpu.make_async_copy(
            asked_ref.at[number], asked_smem.at[number], ask_sems.at[number]
        )
        fetch.start()
        fetch.wait()
        for slot in range(CAP):
            sending[number, slot] = grid_ref[asked_smem[number, 0, slot]]
        copy = pltpu.make_async_remote_copy(
            src_ref=sending.at[number],
            dst_ref=received.at[number],
            send_sem=send_sems.at[number],
            recv_sem=recv_sems.at[number],
            device_id={"nodes": shifted(-offset)},
            device_id_type=pl.DeviceIdType.MESH,
        )
        copy.start()
        copies.append(copy)

    def keep(first, count):
        def store(columns, done):
            keyval[first : first + count, :, columns] = done.astype(keyval.dtype).reshape(
                count, tile_rows, CHUNK
            )

        return store

    loads[1].wait()
    project(
        lambda: grid_ref[...].reshape(own_tiles * tile_rows, width),
        w_keyval_ref,
        keep(0, own_tiles),
    )
    loads[2].wait()

    pair = 1
    for first in range(0, len(offsets), pair):
        for copy in copies[first : first + pair]:
            copy.wait()
        project(
            lambda: received[first : first + pair].reshape(pair * CAP * tile_rows, width),
            w_keyval_ref,
            keep(own_tiles + first * CAP, pair * CAP),
        )

    lane_head = lax.broadcasted_iota(jnp.int32, (1, span), 1) // head_size
    key_slot = lax.broadcasted_iota(jnp.int32, (1, slots * tile_rows), 1) // tile_rows
    for tile in range(mesh_tiles):
        rows = slice(tile * tile_rows, (tile + 1) * tile_rows)
        bias = jnp.zeros((1, slots * tile_rows), jnp.float32)
        for slot in range(slots):
            off = jnp.where(live_ref[tile, slot] > 0, 0.0, -1e30)
            bias = jnp.where(key_slot == slot, off, bias)
        index = [table_ref[tile, slot] for slot in range(slots)]
        for group in range(HEADS // GROUP):
            columns = slice(group * span, (group + 1) * span)
            behind = slice(width + group * span, width + (group + 1) * span)
            query = query_ref[rows, columns]
            stacked = jnp.concatenate(
                [jnp.where(lane_head == h, query, jnp.zeros_like(query)) for h in range(GROUP)],
                axis=0,
            )
            keys = jnp.concatenate([keyval[i, :, columns] for i in index], axis=0)
            values = jnp.concatenate([keyval[i, :, behind] for i in index], axis=0)
            scores = lax.dot_general(
                stacked, keys, (((1,), (1,)), ((), ())), preferred_element_type=jnp.float32
            )
            scores = scores + bias
            raised = jnp.exp(scores - jnp.max(scores, axis=-1, keepdims=True))
            share = 1.0 / jnp.sum(raised, axis=-1, keepdims=True)
            weights = (raised * share).astype(jnp.bfloat16)
            mixed = jnp.dot(weights, values, preferred_element_type=jnp.float32)
            total = jnp.zeros((tile_rows, span), jnp.float32)
            for h in range(GROUP):
                total = jnp.where(
                    lane_head == h, mixed[h * tile_rows : (h + 1) * tile_rows], total
                )
            attended[rows, columns] = total.astype(jnp.bfloat16)
    for part in range(0, width, 512):
        columns = slice(part, part + 512)
        out_ref[:, columns] = mesh_ref[:, columns].astype(jnp.float32) + jnp.dot(
            attended[...], w_out_ref[:, columns], preferred_element_type=jnp.float32
        )


def encode(offsets, request, table, live, grid, mesh_latents, w_query, w_keyval, w_out):
    own_tiles, tile_rows, width = grid.shape
    count = len(offsets)
    vmem = pl.BlockSpec(memory_space=pltpu.VMEM)
    smem = pl.BlockSpec(memory_space=pltpu.SMEM)
    hbm = pl.BlockSpec(memory_space=pl.ANY)
    bf16 = jnp.bfloat16
    return pl.pallas_call(
        functools.partial(encode_kernel, offsets),
        out_shape=jax.ShapeDtypeStruct(mesh_latents.shape, jnp.float32),
        in_specs=[vmem, smem, smem, vmem, vmem, hbm, hbm, hbm],
        out_specs=vmem,
        scratch_shapes=[
            pltpu.VMEM((own_tiles + count * CAP, tile_rows, 2 * width), bf16),
            pltpu.VMEM(mesh_latents.shape, bf16),
            pltpu.VMEM(mesh_latents.shape, bf16),
            pltpu.VMEM((count, CAP, tile_rows, width), bf16),
            pltpu.VMEM((count, CAP, tile_rows, width), bf16),
            pltpu.VMEM(w_query.shape, bf16),
            pltpu.VMEM(w_keyval.shape, bf16),
            pltpu.VMEM(w_out.shape, bf16),
            pltpu.VMEM(request.shape, jnp.int32),
            pltpu.SMEM(request.shape, jnp.int32),
            pltpu.SemaphoreType.DMA((3,)),
            pltpu.SemaphoreType.DMA((count,)),
            pltpu.SemaphoreType.DMA((count,)),
            pltpu.SemaphoreType.DMA((count,)),
            pltpu.SemaphoreType.DMA((count,)),
            pltpu.SemaphoreType.DMA((count,)),
        ],
        compiler_params=pltpu.CompilerParams(
            vmem_limit_bytes=VMEM_LIMIT, collective_id=0, has_side_effects=True
        ),
        name="encode",
    )(request, table, live, grid, mesh_latents, w_query, w_keyval, w_out)


def per_device(
    grid_latents, mesh_latents, neighbour_tiles, neighbour_live, w_query, w_keyval, w_out
):
    width = w_query.shape[0]
    own_tiles = grid_latents.shape[0] // TILE
    node_count = lax.axis_size("nodes")
    position = lax.axis_index("nodes")
    offsets = [sign * o for o in range(1, REACH + 1) for sign in (-1, 1)]

    requests, table = plan_requests(
        neighbour_tiles, neighbour_live, own_tiles, offsets, position, node_count
    )
    request = jnp.pad(jnp.stack(requests)[:, None, :], ((0, 0), (0, 7), (0, 128 - CAP)))
    return encode(
        offsets,
        request,
        table,
        neighbour_live,
        grid_latents.reshape(own_tiles, TILE, width),
        mesh_latents,
        w_query,
        w_keyval,
        w_out,
    )


def solution(mesh):
    return jax.shard_map(
        per_device,
        mesh=mesh,
        in_specs=(
            P(("groups", "nodes"), None),
            P(("groups", "nodes"), None),
            P("nodes", None),
            P("nodes", None),
            P(),
            P(),
            P(),
        ),
        out_specs=P(("groups", "nodes"), None),
        check_vma=False,
    )
```

```python
import functools

import jax
import jax.numpy as jnp
from jax import lax
from jax.experimental import pallas as pl
from jax.experimental.pallas import tpu as pltpu
from jax.sharding import PartitionSpec as P

HEADS = 16
TILE = 128
REACH = 2
CAP = 2
GROUP = 4
CHUNK = 256
VMEM_LIMIT = 52 * 1024 * 1024


def plan_requests(tiles, live, own_tiles, offsets, position, node_count):
    owner = tiles // own_tiles
    local = tiles % own_tiles
    away = (owner - position + node_count + REACH) % node_count - REACH
    ids = jnp.arange(own_tiles, dtype=jnp.int32)
    slot_ids = jnp.arange(CAP, dtype=jnp.int32)
    requests = []
    table = jnp.where(away == 0, local, 0)
    for number, offset in enumerate(offsets):
        wanted = (live > 0) & (away == offset)
        needed = jnp.any(wanted[:, :, None] & (local[:, :, None] == ids), axis=(0, 1))
        before = jnp.sum(
            jnp.where(needed[None, :] & (ids[None, :] < ids[:, None]), 1, 0), axis=1
        )
        chosen = needed[None, :] & (before[None, :] == slot_ids[:, None])
        requests.append(jnp.sum(jnp.where(chosen, ids[None, :], 0), axis=1))
        place = jnp.sum(jnp.where(needed & (ids < local[:, :, None]), 1, 0), axis=2)
        table = jnp.where(wanted, own_tiles + number * CAP + place, table)
    return requests, table


def shifted(offset):
    count = lax.axis_size("nodes")
    return lax.rem(lax.axis_index("nodes") + (offset + count), count)


def project(rows, weight_ref, store):
    @pl.loop(0, weight_ref.shape[1] // CHUNK)
    def _(step):
        columns = pl.ds(pl.multiple_of(step * CHUNK, CHUNK), CHUNK)
        store(
            columns,
            jnp.dot(rows(), weight_ref[:, columns], preferred_element_type=jnp.float32),
        )


def encode_kernel(
    offsets,
    request_ref,
    table_ref,
    live_ref,
    grid_ref,
    mesh_ref,
    w_query_hbm,
    w_keyval_hbm,
    w_out_hbm,
    out_ref,
    keyval,
    query_ref,
    attended,
    sending,
    received,
    w_query_ref,
    w_keyval_ref,
    w_out_ref,
    asked_ref,
    asked_smem,
    weight_sems,
    send_sems,
    recv_sems,
    ask_send_sems,
    ask_recv_sems,
    ask_sems,
):
    own_tiles, tile_rows, width = grid_ref.shape
    head_size = width // HEADS
    span = GROUP * head_size
    mesh_tiles, slots = table_ref.shape

    loads = [
        pltpu.make_async_copy(source, target, weight_sems.at[number])
        for number, (source, target) in enumerate(
            (
                (w_query_hbm, w_query_ref),
                (w_keyval_hbm, w_keyval_ref),
                (w_out_hbm, w_out_ref),
            )
        )
    ]
    for load in loads:
        load.start()

    barrier = pltpu.get_barrier_semaphore()
    for offset in offsets:
        pl.semaphore_signal(
            barrier,
            inc=1,
            device_id={"nodes": shifted(offset)},
            device_id_type=pl.DeviceIdType.MESH,
        )
    pl.semaphore_wait(barrier, len(offsets))

    asks = []
    for number, offset in enumerate(offsets):
        ask = pltpu.make_async_remote_copy(
            src_ref=request_ref.at[number],
            dst_ref=asked_ref.at[number],
            send_sem=ask_send_sems.at[number],
            recv_sem=ask_recv_sems.at[number],
            device_id={"nodes": shifted(offset)},
            device_id_type=pl.DeviceIdType.MESH,
        )
        ask.start()
        asks.append(ask)

    loads[0].wait()

    def store_query(columns, done):
        query_ref[:, columns] = (done * head_size ** (-0.5)).astype(query_ref.dtype)

    project(lambda: mesh_ref[...], w_query_ref, store_query)

    fetches = []
    for number, ask in enumerate(asks):
        ask.wait()
        fetch = pltpu.make_async_copy(
            asked_ref.at[number], asked_smem.at[number], ask_sems.at[number]
        )
        fetch.start()
        fetches.append(fetch)

    copies = []
    for number, offset in enumerate(offsets):
        fetches[number].wait()
        for slot in range(CAP):
            sending[number, slot] = grid_ref[asked_smem[number, 0, slot]]
        copy = pltpu.make_async_remote_copy(
            src_ref=sending.at[number],
            dst_ref=received.at[number],
            send_sem=send_sems.at[number],
            recv_sem=recv_sems.at[number],
            device_id={"nodes": shifted(-offset)},
            device_id_type=pl.DeviceIdType.MESH,
        )
        copy.start()
        copies.append(copy)

    def keep(first, count):
        def store(columns, done):
            keyval[first : first + count, :, columns] = done.astype(keyval.dtype).reshape(
                count, tile_rows, CHUNK
            )

        return store

    loads[1].wait()
    project(
        lambda: grid_ref[...].reshape(own_tiles * tile_rows, width),
        w_keyval_ref,
        keep(0, own_tiles),
    )
    loads[2].wait()

    pair = 1
    for first in range(0, len(offsets), pair):
        for copy in copies[first : first + pair]:
            copy.wait()
        project(
            lambda: received[first : first + pair].reshape(pair * CAP * tile_rows, width),
            w_keyval_ref,
            keep(own_tiles + first * CAP, pair * CAP),
        )

    lane_head = lax.broadcasted_iota(jnp.int32, (1, span), 1) // head_size
    key_slot = lax.broadcasted_iota(jnp.int32, (1, slots * tile_rows), 1) // tile_rows
    for tile in range(mesh_tiles):
        rows = slice(tile * tile_rows, (tile + 1) * tile_rows)
        bias = jnp.zeros((1, slots * tile_rows), jnp.float32)
        for slot in range(slots):
            off = jnp.where(live_ref[tile, slot] > 0, 0.0, -1e30)
            bias = jnp.where(key_slot == slot, off, bias)
        index = [table_ref[tile, slot] for slot in range(slots)]
        for group in range(HEADS // GROUP):
            columns = slice(group * span, (group + 1) * span)
            behind = slice(width + group * span, width + (group + 1) * span)
            query = query_ref[rows, columns]
            stacked = jnp.concatenate(
                [jnp.where(lane_head == h, query, jnp.zeros_like(query)) for h in range(GROUP)],
                axis=0,
            )
            keys = jnp.concatenate([keyval[i, :, columns] for i in index], axis=0)
            values = jnp.concatenate([keyval[i, :, behind] for i in index], axis=0)
            scores = lax.dot_general(
                stacked, keys, (((1,), (1,)), ((), ())), preferred_element_type=jnp.float32
            )
            scores = scores + bias
            raised = jnp.exp(scores - jnp.max(scores, axis=-1, keepdims=True))
            share = 1.0 / jnp.sum(raised, axis=-1, keepdims=True)
            weights = (raised * share).astype(jnp.bfloat16)
            mixed = jnp.dot(weights, values, preferred_element_type=jnp.float32)
            total = jnp.zeros((tile_rows, span), jnp.float32)
            for h in range(GROUP):
                total = jnp.where(
                    lane_head == h, mixed[h * tile_rows : (h + 1) * tile_rows], total
                )
            attended[rows, columns] = total.astype(jnp.bfloat16)
    for part in range(0, width, 512):
        columns = slice(part, part + 512)
        out_ref[:, columns] = mesh_ref[:, columns].astype(jnp.float32) + jnp.dot(
            attended[...], w_out_ref[:, columns], preferred_element_type=jnp.float32
        )


def encode(offsets, request, table, live, grid, mesh_latents, w_query, w_keyval, w_out):
    own_tiles, tile_rows, width = grid.shape
    count = len(offsets)
    vmem = pl.BlockSpec(memory_space=pltpu.VMEM)
    smem = pl.BlockSpec(memory_space=pltpu.SMEM)
    hbm = pl.BlockSpec(memory_space=pl.ANY)
    bf16 = jnp.bfloat16
    return pl.pallas_call(
        functools.partial(encode_kernel, offsets),
        out_shape=jax.ShapeDtypeStruct(mesh_latents.shape, jnp.float32),
        in_specs=[vmem, smem, smem, vmem, vmem, hbm, hbm, hbm],
        out_specs=vmem,
        scratch_shapes=[
            pltpu.VMEM((own_tiles + count * CAP, tile_rows, 2 * width), bf16),
            pltpu.VMEM(mesh_latents.shape, bf16),
            pltpu.VMEM(mesh_latents.shape, bf16),
            pltpu.VMEM((count, CAP, tile_rows, width), bf16),
            pltpu.VMEM((count, CAP, tile_rows, width), bf16),
            pltpu.VMEM(w_query.shape, bf16),
            pltpu.VMEM(w_keyval.shape, bf16),
            pltpu.VMEM(w_out.shape, bf16),
            pltpu.VMEM(request.shape, jnp.int32),
            pltpu.SMEM(request.shape, jnp.int32),
            pltpu.SemaphoreType.DMA((3,)),
            pltpu.SemaphoreType.DMA((count,)),
            pltpu.SemaphoreType.DMA((count,)),
            pltpu.SemaphoreType.DMA((count,)),
            pltpu.SemaphoreType.DMA((count,)),
            pltpu.SemaphoreType.DMA((count,)),
        ],
        compiler_params=pltpu.CompilerParams(
            vmem_limit_bytes=VMEM_LIMIT, collective_id=0, has_side_effects=True
        ),
        name="encode",
    )(request, table, live, grid, mesh_latents, w_query, w_keyval, w_out)


def per_device(
    grid_latents, mesh_latents, neighbour_tiles, neighbour_live, w_query, w_keyval, w_out
):
    width = w_query.shape[0]
    own_tiles = grid_latents.shape[0] // TILE
    node_count = lax.axis_size("nodes")
    position = lax.axis_index("nodes")
    offsets = [sign * o for o in range(1, REACH + 1) for sign in (-1, 1)]

    requests, table = plan_requests(
        neighbour_tiles, neighbour_live, own_tiles, offsets, position, node_count
    )
    request = jnp.pad(jnp.stack(requests)[:, None, :], ((0, 0), (0, 7), (0, 128 - CAP)))
    return encode(
        offsets,
        request,
        table,
        neighbour_live,
        grid_latents.reshape(own_tiles, TILE, width),
        mesh_latents,
        w_query,
        w_keyval,
        w_out,
    )


def solution(mesh):
    return jax.shard_map(
        per_device,
        mesh=mesh,
        in_specs=(
            P(("groups", "nodes"), None),
            P(("groups", "nodes"), None),
            P("nodes", None),
            P("nodes", None),
            P(),
            P(),
            P(),
        ),
        out_specs=P(("groups", "nodes"), None),
        check_vma=False,
    )
```
